32 devices in a mesh: dp: 8 (over y, x, core), node: 4 (over z).
Axes of the slice: x: 2, y: 2, z: 4, core: 2. Of those that a mesh axis runs over, the one named last changes fastest.
Arguments:
- hidden_in: bfloat16 [8192, 8192], P(('dp', 'node')), may hold values from -6 to 6
- norm_gain: bfloat16 [8192], replicated, may hold values from 0.5 to 1.5
- weight_codes: bfloat16 [8192, 1024], P('node'), may hold values from -127 to 127
- weight_scales: float32 [8192, 4], P('node'), may hold values from 6.90534e-05 to 0.00069053395
- cotangent: bfloat16 [8192, 1024], P(('dp', 'node')), may hold values from -6 to 6
Outputs:
- values: bfloat16 [8192, 1024], P(('dp', 'node'))
- input_gradient: bfloat16 [8192, 8192], P(('dp', 'node'))
- weight_grad: float32 [8192, 1024], P(('dp', 'node'))
- gain_gradient_mean: float32 [8192], replicated
The draws below stay inside these ranges and needn't reach their ends.
All inputs are finite; a program needn't handle non-finite values.
Results may differ from the reference program's by a relative error of at most 0.014.
Values may be sent and summed in bfloat16 or wider, within the bound.
No kernel may reach another device: no remote copies, remote signals or barrier semaphores. Data moves between devices by JAX's collectives and lax.ppermute only.
A program may use at most 256 MiB of HBM per device.

```python
import math
import jax
import jax.numpy as jnp
from jax import lax

D = 8192
KV = 1024
BLOCK = 256
TOK_DEV = 256
TOKENS = 8192
N_DP = 8
N_NODE = 4


def steps_of(own_key, dims, pieces, smallest, high):
    def one(axis_at, blocks):
        steps = jax.random.uniform(jax.random.fold_in(jax.random.fold_in(own_key, 6), axis_at), (blocks,), jnp.float32, smallest / len(pieces), high / len(pieces))
        return jnp.repeat(jnp.exp(steps), dims[axis_at] // blocks).reshape((-1,) + (1,) * (len(dims) - axis_at - 1))

    factor_of = one(*pieces[0])
    for cut in pieces[1:]:
        factor_of = factor_of * one(*cut)
    return factor_of


def scatter_about(rng, dims, spread, limit, split=(), dtype=jnp.bfloat16):
    array = jax.random.normal(rng, dims, jnp.float32) * spread
    if len(split) > 0:
        array = steps_of(rng, dims, split, -0.22, 0.18) * array
    return jnp.clip(array, min=-limit, max=limit).astype(dtype)


def setup_inputs(seed: int = 0) -> dict:
    keys = jax.random.split(jax.random.key(seed), 6)
    return {
        "hidden_in": scatter_about(keys[0], (TOKENS, D), 1.0, 6.0, ((0, 32),)),
        "norm_gain": jnp.clip(1.0 + 0.1 * jax.random.normal(keys[1], (D,), jnp.float32), 0.5, 1.5).astype(jnp.bfloat16),
        "weight_codes": scatter_about(keys[2], (D, KV), 40.0, 127.0, ((0, 4),)),
        "weight_scales": jnp.clip(jnp.exp(math.log(0.00069053395) - 2.30258503 * jax.random.uniform(keys[3], (D, KV // BLOCK), jnp.float32) ** steps_of(keys[3], (D, KV // BLOCK), ((0, 4),), -0.2, 0.2)), 6.90533997840248e-05, 0.00069053395),
        "cotangent": scatter_about(keys[4], (TOKENS, KV), 1.0, 6.0, ((0, 32),)),
    }


def quantize(blocks):
    scale = (jnp.sqrt(lax.optimization_barrier(jnp.mean(blocks * blocks, axis=-1, keepdims=True)) + 1e-06) / 3.5).astype(jnp.bfloat16)
    scale = lax.optimization_barrier(scale)
    wide = scale.astype(jnp.float32)
    codes = jnp.clip(blocks / wide, -7.0, 7.0).astype(jnp.bfloat16)
    return (codes, scale)

def restore(codes, scale):
    return codes.astype(jnp.float32) * scale.astype(jnp.float32)

def requantized(matrix):
    blocks = matrix.reshape(D, KV // BLOCK, BLOCK)
    codes, scale = quantize(blocks)
    return restore(codes, scale).reshape(D, KV)

def reference(hidden_in, norm_gain, weight_codes, weight_scales, cotangent):
    input_broadcast = hidden_in.astype(jnp.float32)
    inverse_deviation = lax.rsqrt(lax.optimization_barrier(jnp.mean(input_broadcast * input_broadcast, axis=-1, keepdims=True)) + 1e-05)
    centered_unit_rows = input_broadcast * inverse_deviation
    gain_broadcast = norm_gain.astype(jnp.float32)
    normed_rows = (centered_unit_rows * gain_broadcast).astype(jnp.bfloat16)
    weight = (weight_codes.astype(jnp.float32).reshape(D, KV // BLOCK, BLOCK) * weight_scales[:, :, None]).reshape(D, KV).astype(jnp.bfloat16)
    values = jnp.dot(normed_rows, weight, preferred_element_type=jnp.float32).astype(jnp.bfloat16)
    normed_gradient = jnp.dot(cotangent, weight.T, preferred_element_type=jnp.float32).astype(jnp.bfloat16)
    gain_scaled_rows = gain_broadcast * normed_gradient.astype(jnp.float32)
    input_gradient = (inverse_deviation * (gain_scaled_rows - centered_unit_rows * lax.optimization_barrier(jnp.mean(gain_scaled_rows * centered_unit_rows, axis=-1, keepdims=True)))).astype(jnp.bfloat16)
    device_list = N_DP * N_NODE
    gain_gradient_mean = lax.optimization_barrier(jnp.sum(normed_gradient.astype(jnp.float32) * centered_unit_rows, axis=0)) / device_list
    normed_blocks = normed_rows.reshape(N_DP, N_NODE, TOK_DEV, D)
    cot_blocks = cotangent.reshape(N_DP, N_NODE, TOK_DEV, KV)

    def node_section(acc, pair):
        rows_in, cot_in = pair
        partial_value = jnp.dot(rows_in.T, cot_in, preferred_element_type=jnp.float32)
        return (acc + requantized(partial_value), None)

    def data_section(total, pair):
        rows_group, cot_group = pair
        node_sum, unused = lax.scan(node_section, jnp.zeros((D, KV), jnp.float32), (rows_group, cot_group))
        return (total + requantized(node_sum), None)
    total, unused = lax.scan(data_section, jnp.zeros((D, KV), jnp.float32), (normed_blocks, cot_blocks))
    weight_grad = total / device_list
    return (values, input_gradient, weight_grad, gain_gradient_mean)
```

```python
import functools

import jax
import jax.numpy as jnp
from jax import lax
from jax.experimental import pallas as pl
from jax.experimental.pallas import tpu as pltpu
from jax.sharding import PartitionSpec as P

BLOCK = 256
CHUNKS = 2
F32 = jnp.float32
BF16 = jnp.bfloat16
VMEM = pl.BlockSpec(memory_space=pltpu.VMEM)
SMEM = pl.BlockSpec(memory_space=pltpu.SMEM)
PARAMS = pltpu.CompilerParams(vmem_limit_bytes=56 * 1024 * 1024)


def scaled(codes, scales):
    parts = [
        (codes[:, j * BLOCK : (j + 1) * BLOCK].astype(F32) * scales[:, j : j + 1]).astype(BF16)
        for j in range(codes.shape[1] // BLOCK)
    ]
    return jnp.concatenate(parts, axis=1)


def clipped(block):
    mean = jnp.mean(block * block, axis=-1, keepdims=True)
    limit = 7.0 * (jnp.sqrt(mean + 1e-06) * (1.0 / 3.5)).astype(BF16).astype(F32)
    return jnp.clip(block, -limit, limit)


def piece_kernel(which, codes, scales, cot, out):
    rows = codes.shape[0]
    out[:rows, :] = scaled(codes[...], scales[...])
    out[rows:, :] = cot[...]


def weight_piece(which, codes, scales, cot, rows):
    tokens, kv = cot.shape
    return pl.pallas_call(
        piece_kernel,
        grid_spec=pltpu.PrefetchScalarGridSpec(
            num_scalar_prefetch=1,
            grid=(1,),
            in_specs=[
                pl.BlockSpec((rows, kv), lambda i, w: (w[0], 0)),
                pl.BlockSpec((rows, scales.shape[1]), lambda i, w: (w[0], 0)),
                pl.BlockSpec((tokens, kv), lambda i, w: (0, 0)),
            ],
            out_specs=pl.BlockSpec((rows + tokens, kv), lambda i, w: (0, 0)),
        ),
        out_shape=jax.ShapeDtypeStruct((rows + tokens, kv), BF16),
        compiler_params=PARAMS,
        name="weight_piece",
    )(which, codes, scales, cot)


def norm_kernel(n, m, me, hidden, gain, *rest):
    outs, rstd, turned = rest[:-2], rest[-2], rest[-1]
    tokens, d = hidden.shape
    own = d // (n * m)
    part = own // CHUNKS
    wide = 512

    def square(i, total):
        h = hidden[:, pl.ds(pl.multiple_of(i * wide, wide), wide)].astype(F32)
        return total + jnp.sum(h * h, axis=-1, keepdims=True)

    total = lax.fori_loop(0, d // wide, square, jnp.zeros((tokens, 1), F32))
    inverse = lax.rsqrt(total * (1.0 / d) + 1e-05)
    rstd[...] = jnp.broadcast_to(inverse, rstd.shape)

    def turn(i, carry):
        at = pl.ds(pl.multiple_of(i * 256, 256), 256)
        x = hidden[:, at].astype(F32) * inverse * gain[:, at]
        turned[at, :] = x.astype(BF16).T
        return carry

    lax.fori_loop(0, d // 256, turn, 0)
    for s in range(n):
        to = lax.rem(me[0] + s, n)
        for k in range(CHUNKS):
            out = outs[s * CHUNKS + k]
            for a in range(m):
                start = pl.multiple_of((a * n + to) * own + k * part, part)
                out[a * part : (a + 1) * part, :] = turned[pl.ds(start, part), :]


def norm_rows(me, hidden, gain, n, m):
    tokens, d = hidden.shape
    part = jax.ShapeDtypeStruct((d // (n * CHUNKS), tokens), BF16)
    got = pl.pallas_call(
        functools.partial(norm_kernel, n, m),
        in_specs=[SMEM, VMEM, VMEM],
        out_specs=[VMEM] * (n * CHUNKS + 1),
        out_shape=[part] * (n * CHUNKS) + [jax.ShapeDtypeStruct((tokens, 128), F32)],
        scratch_shapes=[pltpu.VMEM((d, tokens), BF16)],
        compiler_params=PARAMS,
        name="norm_rows",
    )(me, hidden, gain)
    sends = [got[s * CHUNKS : (s + 1) * CHUNKS] for s in range(n)]
    return sends, got[-1]


def grad_kernel(n, *refs):
    rows, cots, out = refs[:n], refs[n : 2 * n], refs[2 * n]
    kv = out.shape[1]
    for j in range(kv // BLOCK):
        at = slice(j * BLOCK, (j + 1) * BLOCK)
        total = None
        for s in range(n):
            term = clipped(jnp.dot(rows[s][...], cots[s][:, at], preferred_element_type=F32))
            total = term if total is None else total + term
        out[:, at] = clipped(total).astype(BF16)


def node_sum(rows, cots):
    n = len(rows)
    count, tokens = rows[0].shape
    kv = cots[0].shape[1]
    tile = min(128, count)
    return pl.pallas_call(
        functools.partial(grad_kernel, n),
        grid=(count // tile,),
        in_specs=[pl.BlockSpec((tile, tokens), lambda i: (i, 0))] * n
        + [pl.BlockSpec((tokens, kv), lambda i: (0, 0))] * n,
        out_specs=pl.BlockSpec((tile, kv), lambda i: (i, 0)),
        out_shape=jax.ShapeDtypeStruct((count, kv), BF16),
        compiler_params=PARAMS,
        cost_estimate=pl.CostEstimate(
            flops=2 * n * count * tokens * kv,
            bytes_accessed=n * count * tokens * 2 + n * tokens * kv * 2 + count * kv * 2,
            transcendentals=0,
        ),
        name="node_sum",
    )(*rows, *cots)


def project(starts, hidden, gain, rstd, cot, weights, first, values, gains, mean, keep):
    at_start = first
    for array, load in weights:
        rows = array.shape[0]
        tile = min(256, rows)
        for j in range(rows // tile):
            start = pl.multiple_of(starts[at_start] + j * tile, 128)
            at = pl.ds(start, tile)
            w = load(j * tile, tile)
            g = gain[:, at]
            xhat = hidden[:, at].astype(F32) * rstd
            normed = (xhat * g).astype(BF16)
            values[...] += jnp.dot(normed, w, preferred_element_type=F32)
            grad = lax.dot_general(
                cot[...], w, (((1,), (1,)), ((), ())), preferred_element_type=F32
            ).astype(BF16)
            keep(at_start, j * tile, tile, grad)
            product = grad.astype(F32) * xhat
            gains[:, at] = jnp.sum(product, axis=0, keepdims=True)
            mean[...] += jnp.sum(product * g, axis=-1, keepdims=True)
        at_start += 1


def own_kernel(starts, hidden, gain, rstd, cot, codes, scales, values, gains, mean, grads):
    values[...] = jnp.zeros_like(values)
    mean[...] = jnp.zeros_like(mean)

    def load(first, count):
        return scaled(codes[first : first + count, :], scales[first : first + count, :])

    def keep(which, first, count, grad):
        grads[:, first : first + count] = grad

    project(starts, hidden, gain, rstd[:, :1], cot, [(codes, load)], 0, values, gains, mean, keep)


def own_part(starts, hidden, gain, rstd, cot, codes, scales):
    tokens, d = hidden.shape
    kv = cot.shape[1]
    return pl.pallas_call(
        own_kernel,
        in_specs=[SMEM] + [VMEM] * 6,
        out_specs=[VMEM] * 4,
        out_shape=[
            jax.ShapeDtypeStruct((tokens, kv), F32),
            jax.ShapeDtypeStruct((1, d), F32),
            jax.ShapeDtypeStruct((tokens, 128), F32),
            jax.ShapeDtypeStruct((tokens, codes.shape[0]), BF16),
        ],
        compiler_params=PARAMS,
        cost_estimate=pl.CostEstimate(
            flops=4 * tokens * codes.shape[0] * kv,
            bytes_accessed=12 * 1024 * 1024,
            transcendentals=0,
        ),
        name="own_part",
    )(starts, hidden, gain, rstd, cot, codes, scales)


def rest_kernel(count, starts, hidden, gain, rstd, cot, values_in, gains_in, mean_in, own_grads, *refs):
    weights, (values, gains, result, total, mean, grads) = refs[:count], refs[count:]
    total[...] = values_in[...]
    gains[...] = gains_in[...]
    mean[...] = mean_in[...]
    inverse = rstd[:, :1]
    rows = weights[0].shape[0]

    def keep(which, first, size, grad):
        at = (which - 1) * rows + first
        grads[:, at : at + size] = grad

    listed = [(w, functools.partial(lambda w, first, size: w[first : first + size, :], w)) for w in weights]
    project(starts, hidden, gain, inverse, cot, listed, 1, total, gains, mean, keep)
    values[...] = total[...].astype(BF16)
    center = mean[:, :1] * (1.0 / hidden.shape[1])

    def finish(start, size, grad):
        at = pl.ds(pl.multiple_of(start, 128), size)
        xhat = hidden[:, at].astype(F32) * inverse
        t = gain[:, at] * grad.astype(F32)
        result[:, at] = (inverse * (t - xhat * center)).astype(BF16)

    for j in range(own_grads.shape[1] // 128):
        finish(starts[0] + j * 128, 128, own_grads[:, j * 128 : (j + 1) * 128])
    for i in range(count):
        for j in range(rows // 128):
            at = i * rows + j * 128
            finish(starts[i + 1] + j * 128, 128, grads[:, at : at + 128])


def rest_part(starts, hidden, gain, rstd, cot, own, weights):
    tokens, d = hidden.shape
    kv = cot.shape[1]
    count = len(weights)
    width = count * weights[0].shape[0]
    return pl.pallas_call(
        functools.partial(rest_kernel, count),
        in_specs=[SMEM] + [VMEM] * (8 + count),
        out_specs=[VMEM] * 3,
        out_shape=[
            jax.ShapeDtypeStruct((tokens, kv), BF16),
            jax.ShapeDtypeStruct((1, d), F32),
            jax.ShapeDtypeStruct((tokens, d), BF16),
        ],
        scratch_shapes=[
            pltpu.VMEM((tokens, kv), F32),
            pltpu.VMEM((tokens, 128), F32),
            pltpu.VMEM((tokens, width), BF16),
        ],
        compiler_params=PARAMS,
        cost_estimate=pl.CostEstimate(
            flops=4 * tokens * width * kv,
            bytes_accessed=(width * kv + 3 * tokens * d) * 2,
            transcendentals=0,
        ),
        name="rest_part",
    )(starts, hidden, gain, rstd, cot, *own, *weights)


def pair_sum(parts):
    while len(parts) > 1:
        parts = [parts[i] + parts[i + 1] for i in range(0, len(parts), 2)]
    return parts[0]


def exchange_sum(value, axis, size):
    def flip(bit):
        return lax.ppermute(value, axis, [(i, i ^ bit) for i in range(size)])

    return pair_sum([value] + [flip(bit) for bit in range(1, size)])


def local(hidden, gain, codes, scales, cot):
    m, n = lax.axis_size("dp"), lax.axis_size("node")
    a, z = lax.axis_index("dp"), lax.axis_index("node")
    tokens, d = hidden.shape
    kv = cot.shape[1]
    own = d // (m * n)
    pieces = min(m, d // n // 128)
    size = d // n // pieces
    gain = gain.astype(F32).reshape(1, d)
    here = lax.rem(a, pieces)

    chain = weight_piece(here.reshape(1), codes, scales, cot, size)
    up, down = [chain], [chain]
    for s in range(1, n):
        up.append(lax.ppermute(up[-1], "node", [(i, i + 1) for i in range(s - 1, n - 1)]))
        down.append(lax.ppermute(down[-1], "node", [(i + 1, i) for i in range(n - s)]))

    sends, rstd = norm_rows(z.reshape(1), hidden, gain, n, m)
    got = [sends[0]]
    for s in range(1, n):
        shift = [(i, (i + s) % n) for i in range(n)]
        got.append([lax.ppermute(x, "node", shift) for x in sends[s]])

    starts = [z * (d // n)]
    weights, cots = [], [cot]
    odd = []
    for s in range(1, n):
        slot = jnp.where(z >= s, up[s], down[n - s])
        cots.append(slot[size:])
        mine = slot[:size]
        source = lax.rem(z + n - s, n) * (d // n)
        for bit in range(0, pieces, 2):
            part = mine
            if bit:
                part = lax.ppermute(mine, "dp", [(i, i ^ bit) for i in range(m)])
            weights.append(part)
            starts.append(source + lax.bitwise_xor(here, bit) * size)
            odd.append(
                (lax.ppermute(part, "dp", [(i, i ^ 1) for i in range(m)]), source + lax.bitwise_xor(here, bit + 1) * size)
            )
    weights += [w for w, _ in odd]
    starts = jnp.stack(starts + [at for _, at in odd]).astype(jnp.int32)

    first = own_part(starts, hidden, gain, rstd, cot, codes, scales)
    values, gains, input_gradient = rest_part(starts, hidden, gain, rstd, cot, first, weights)
    gains = exchange_sum(exchange_sum(gains, "node", n), "dp", m)
    gain_gradient_mean = gains.reshape(d) * (1.0 / (m * n))

    done = []
    for k in range(CHUNKS):
        total = node_sum([g[k] for g in got], cots)
        back = lax.all_to_all(total.reshape(m, own // CHUNKS, kv), "dp", split_axis=0, concat_axis=0, tiled=True)
        done.append(jnp.sum(back.astype(F32), axis=0) * (1.0 / (m * n)))
    weight_grad = jnp.concatenate(done, axis=0)
    return (values, input_gradient, weight_grad, gain_gradient_mean)


def solution(mesh):
    rows = P(("dp", "node"), None)
    return jax.shard_map(
        local,
        mesh=mesh,
        in_specs=(rows, P(), P("node", None), P("node", None), rows),
        out_specs=(rows, rows, rows, P()),
        check_vma=False,
    )
```

```python
import functools

import jax
import jax.numpy as jnp
from jax import lax
from jax.experimental import pallas as pl
from jax.experimental.pallas import tpu as pltpu
from jax.sharding import PartitionSpec as P

BLOCK = 256
CUTS = (2, 2, 2, 2)
F32 = jnp.float32
BF16 = jnp.bfloat16
VMEM = pl.BlockSpec(memory_space=pltpu.VMEM)
SMEM = pl.BlockSpec(memory_space=pltpu.SMEM)
CHEAP = pl.CostEstimate(flops=1000, bytes_accessed=1000, transcendentals=0)
PARAMS = pltpu.CompilerParams(vmem_limit_bytes=56 * 1024 * 1024)


def cuts(own):
    unit = own // sum(CUTS)
    sizes = [unit * c for c in CUTS]
    sizes = [x for x in sizes if x]
    return [(sum(sizes[:k]), size) for k, size in enumerate(sizes)]


def scaled(codes, scales):
    parts = [
        (codes[:, j * BLOCK : (j + 1) * BLOCK].astype(F32) * scales[:, j : j + 1]).astype(BF16)
        for j in range(codes.shape[1] // BLOCK)
    ]
    return jnp.concatenate(parts, axis=1)


def clipped(block):
    mean = jnp.sum(block * block, axis=-1, keepdims=True) * (1.0 / BLOCK) + 1e-06
    limit = 7.0 * (mean * lax.rsqrt(mean) * (1.0 / 3.5)).astype(BF16).astype(F32)
    return jnp.clip(block, -limit, limit)


def piece_kernel(which, codes, scales, cot, out):
    tokens = cot.shape[0]
    out[:tokens, :] = cot[...]
    out[tokens:, :] = scaled(codes[...], scales[...].T)


def weight_piece(which, codes, scales, cot, rows):
    tokens, kv = cot.shape
    return pl.pallas_call(
        piece_kernel,
        grid_spec=pltpu.PrefetchScalarGridSpec(
            num_scalar_prefetch=1,
            grid=(1,),
            in_specs=[
                pl.BlockSpec((rows, kv), lambda i, w: (w[0], 0)),
                pl.BlockSpec((scales.shape[0], rows), lambda i, w: (0, w[0])),
                pl.BlockSpec((tokens, kv), lambda i, w: (0, 0)),
            ],
            out_specs=pl.BlockSpec((tokens + rows, kv), lambda i, w: (0, 0)),
        ),
        out_shape=jax.ShapeDtypeStruct((tokens + rows, kv), BF16),
        compiler_params=PARAMS,
        cost_estimate=CHEAP,
        name="weight_piece",
    )(which, codes, scales, cot)


def norm_kernel(n, m, hidden, gain, after, *rest):
    outs, rstd, turned = rest[:-2], rest[-2], rest[-1]
    tokens, d = hidden.shape
    own = d // (n * m)
    wide = 512

    def square(i, total):
        h = hidden[:, pl.ds(pl.multiple_of(i * wide, wide), wide)].astype(F32)
        return total + jnp.sum(h * h, axis=-1, keepdims=True)

    total = lax.fori_loop(0, d // wide, square, jnp.zeros((tokens, 1), F32))
    inverse = lax.rsqrt(total * (1.0 / d) + 1e-05)
    rstd[...] = jnp.broadcast_to(inverse, rstd.shape)

    def turn(i, carry):
        at = pl.ds(pl.multiple_of(i * 256, 256), 256)
        x = hidden[:, at].astype(F32) * inverse * gain[:, at]
        turned[at, :] = x.astype(BF16).T
        return carry

    lax.fori_loop(0, d // 256, turn, 0)
    for k, (first, part) in enumerate(cuts(own)):
        for z in range(n):
            for a in range(m):
                start = (a * n + z) * own + first
                outs[k][z, a * part : (a + 1) * part, :] = turned[start : start + part, :]


def norm_rows(hidden, gain, after, n, m):
    tokens, d = hidden.shape
    parts = [jax.ShapeDtypeStruct((n, m * part, tokens), BF16) for _, part in cuts(d // (n * m))]
    got = pl.pallas_call(
        functools.partial(norm_kernel, n, m),
        in_specs=[VMEM, VMEM, pl.BlockSpec(memory_space=pl.ANY)],
        out_specs=[VMEM] * (len(parts) + 1),
        out_shape=parts + [jax.ShapeDtypeStruct((tokens, 128), F32)],
        scratch_shapes=[pltpu.VMEM((d, tokens), BF16)],
        compiler_params=PARAMS,
        cost_estimate=CHEAP,
        name="norm_rows",
    )(hidden, gain, after)
    return list(got[:-1]), got[-1]


def grad_kernel(n, m, count, me, rows, *refs):
    cots, outs = refs[:n], refs[n + count :]
    part = rows.shape[1] // m
    for which, out in enumerate(outs):
        owners = [lax.bitwise_xor(me[1], p) * 2 + me[2 + which] for p in range(m // 2)]
        lhs = []
        for s in range(n):
            source = lax.rem(me[0] + n - s, n)
            lhs.append(
                jnp.concatenate(
                    [rows[source, pl.ds(pl.multiple_of(o * part, part), part), :] for o in owners], axis=0
                )
            )
        for j in range(out.shape[1] // BLOCK):
            at = slice(j * BLOCK, (j + 1) * BLOCK)
            total = None
            for s in range(n):
                term = clipped(jnp.dot(lhs[s], cots[s][:, at], preferred_element_type=F32))
                total = term if total is None else total + term
            out[:, at] = clipped(total).astype(BF16)


def node_sum(z, chip, cores, rows, cots, m, after):
    n, count, tokens = rows.shape
    kv = cots[0].shape[1]
    return pl.pallas_call(
        functools.partial(grad_kernel, n, m, len(after)),
        grid=(1,),
        in_specs=[SMEM, VMEM]
        + [pl.BlockSpec((tokens, kv), lambda i: (0, 0))] * n
        + [pl.BlockSpec(memory_space=pl.ANY)] * len(after),
        out_specs=[VMEM] * len(cores),
        out_shape=[jax.ShapeDtypeStruct((count // 2, kv), BF16)] * len(cores),
        compiler_params=PARAMS,
        cost_estimate=CHEAP,
        name="node_sum",
    )(jnp.stack([z, chip, *cores]).astype(jnp.int32), rows, *cots, *after)


def project(starts, hidden, gain, rstd, cot, weights, values, gains, mean, keep):
    for which, (tile, count, load) in enumerate(weights):
        for j in range(count):
            w = load(j * tile, tile)
            at = pl.ds(pl.multiple_of(starts[which, j], 128), tile)
            g = gain[:, at]
            xhat = hidden[:, at].astype(F32) * rstd
            normed = (xhat * g).astype(BF16)
            values[...] += jnp.dot(normed, w, preferred_element_type=F32)
            grad = lax.dot_general(
                cot[...], w, (((1,), (1,)), ((), ())), preferred_element_type=F32
            ).astype(BF16)
            keep(which, j, tile, grad)
            product = grad.astype(F32) * xhat
            gains[:, at] = jnp.sum(product, axis=0, keepdims=True)
            mean[...] += jnp.sum(product * g, axis=-1, keepdims=True)


def own_kernel(starts, hidden, gain, rstd, cot, codes, scales, after, values, gains, mean, grads):
    values[...] = jnp.zeros_like(values)
    mean[...] = jnp.zeros_like(mean)
    gains[...] = jnp.zeros_like(gains)
    tile = 256
    count = codes.shape[0] // tile

    def load(first, size):
        return scaled(codes[first : first + size, :], scales[:, first : first + size].T)

    def keep(which, j, size, grad):
        grads[:, j * size : (j + 1) * size] = grad

    project(starts, hidden, gain, rstd[:, :1], cot, [(tile, count, load)], values, gains, mean, keep)


def part_shapes(tokens, kv, d, width):
    return [
        jax.ShapeDtypeStruct((tokens, kv), F32),
        jax.ShapeDtypeStruct((1, d), F32),
        jax.ShapeDtypeStruct((tokens, 128), F32),
        jax.ShapeDtypeStruct((tokens, width), BF16),
    ]


def own_part(starts, hidden, gain, rstd, cot, codes, scales, after):
    tokens, d = hidden.shape
    return pl.pallas_call(
        own_kernel,
        in_specs=[SMEM] + [VMEM] * 6 + [pl.BlockSpec(memory_space=pl.ANY)],
        out_specs=[VMEM] * 4,
        out_shape=part_shapes(tokens, cot.shape[1], d, codes.shape[0]),
        compiler_params=PARAMS,
        cost_estimate=CHEAP,
        name="own_part",
    )(starts, hidden, gain, rstd, cot, codes, scales, after)


def listed(weights, slot):
    return [
        (slot, w.shape[0] // slot, functools.partial(lambda w, first, size: w[first : first + size, :], w))
        for w in weights
    ]


def more_kernel(count, slot, starts, hidden, gain, rstd, cot, values_in, gains_in, mean_in, *refs):
    weights, (values, gains, mean, grads) = refs[:count], refs[count:]
    values[...] = values_in[...]
    gains[...] = gains_in[...]
    mean[...] = mean_in[...]
    width = weights[0].shape[0]

    def keep(which, j, size, grad):
        grads[:, which * width + j * size : which * width + (j + 1) * size] = grad

    project(starts, hidden, gain, rstd[:, :1], cot, listed(weights, slot), values, gains, mean, keep)


def more_part(starts, hidden, gain, rstd, cot, sums, weights, slot):
    tokens, d = hidden.shape
    count = len(weights)
    return pl.pallas_call(
        functools.partial(more_kernel, count, slot),
        in_specs=[SMEM] + [VMEM] * (7 + count),
        out_specs=[VMEM] * 4,
        out_shape=part_shapes(tokens, cot.shape[1], d, count * weights[0].shape[0]),
        compiler_params=PARAMS,
        cost_estimate=CHEAP,
        name="more_part",
    )(starts, hidden, gain, rstd, cot, *sums, *weights)


def last_kernel(count, kept, slot, *refs):
    starts, others, refs = refs[0], refs[1 : 1 + kept], refs[1 + kept :]
    hidden, gain, rstd, cot, values_in, gains_in, mean_in = refs[:7]
    olds, weights = refs[7 : 7 + kept], refs[7 + kept : 7 + kept + count]
    values, gains, result, total, mean, grads = refs[7 + kept + count :]
    total[...] = values_in[...]
    gains[...] = gains_in[...]
    mean[...] = mean_in[...]
    inverse = rstd[:, :1]
    width = weights[0].shape[0]

    def keep(which, j, size, grad):
        grads[:, which * width + j * size : which * width + (j + 1) * size] = grad

    project(starts, hidden, gain, inverse, cot, listed(weights, slot), total, gains, mean, keep)
    values[...] = total[...].astype(BF16)
    center = mean[:, :1] * (1.0 / hidden.shape[1])

    def finish(start, grad):
        at = pl.ds(pl.multiple_of(start, 128), grad.shape[1])
        xhat = hidden[:, at].astype(F32) * inverse
        t = gain[:, at] * grad.astype(F32)
        result[:, at] = (inverse * (t - xhat * center)).astype(BF16)

    for at, old in list(zip(others, olds)) + [(starts, grads)]:
        size = old.shape[1] // (at.shape[0] * at.shape[1])
        for i in range(at.shape[0]):
            for j in range(at.shape[1]):
                first = (i * at.shape[1] + j) * size
                finish(at[i, j], old[:, first : first + size])


def last_part(starts, others, hidden, gain, rstd, cot, sums, olds, weights, slot):
    tokens, d = hidden.shape
    kv = cot.shape[1]
    count, kept = len(weights), len(olds)
    return pl.pallas_call(
        functools.partial(last_kernel, count, kept, slot),
        in_specs=[SMEM] * (1 + kept) + [VMEM] * (7 + kept + count),
        out_specs=[VMEM] * 3,
        out_shape=[
            jax.ShapeDtypeStruct((tokens, kv), BF16),
            jax.ShapeDtypeStruct((1, d), F32),
            jax.ShapeDtypeStruct((tokens, d), BF16),
        ],
        scratch_shapes=[
            pltpu.VMEM((tokens, kv), F32),
            pltpu.VMEM((tokens, 128), F32),
            pltpu.VMEM((tokens, count * weights[0].shape[0]), BF16),
        ],
        compiler_params=PARAMS,
        cost_estimate=CHEAP,
        name="last_part",
    )(starts, *others, hidden, gain, rstd, cot, *sums, *olds, *weights)


def gate(arrays, after):
    count = len(arrays)
    anywhere = pl.BlockSpec(memory_space=pl.ANY)
    return pl.pallas_call(
        lambda *refs: None,
        in_specs=[anywhere] * (count + len(after)),
        out_specs=[anywhere] * count,
        out_shape=[jax.ShapeDtypeStruct(x.shape, x.dtype) for x in arrays],
        input_output_aliases={i: i for i in range(count)},
        name="gate",
    )(*arrays, *after)


def pair_sum(parts):
    while len(parts) > 1:
        parts = [parts[i] + parts[i + 1] for i in range(0, len(parts), 2)]
    return parts[0]


def exchange_sum(value, axis, size, first, last):
    for step in range(first, last):
        value = value + lax.ppermute(value, axis, [(i, i ^ (1 << step)) for i in range(size)])
    return value


def ring(value, n):
    def shift(x, by):
        return lax.ppermute(x, "node", [(i, (i + by) % n) for i in range(n)])

    slots, up, down = {}, value, value
    for s in range(1, n // 2 + 1):
        up = slots[s] = shift(up, 1)
        if n - s > s:
            down = slots[n - s] = shift(down, -1)
    return slots


def local(hidden, gain, codes, scales, cot):
    m, n = lax.axis_size("dp"), lax.axis_size("node")
    a, z = lax.axis_index("dp"), lax.axis_index("node")
    tokens, d = hidden.shape
    kv = cot.shape[1]
    own = d // (m * n)
    pieces = min(m, d // n // 128)
    size = d // n // pieces
    gain = gain.astype(F32).reshape(1, d)
    scales = scales.T
    here = lax.rem(a, pieces)
    chip, core = lax.div(a, 2), lax.rem(a, 2)

    def flip(value, bits):
        return lax.ppermute(value, "dp", [(i, i ^ bits[i % 2]) for i in range(m)])

    piece = weight_piece(here.reshape(1), codes, scales, cot, size)
    sends, rstd = norm_rows(hidden, gain, piece, n, m)
    own_start = (z * (d // n) + jnp.arange(d // n // 256, dtype=jnp.int32) * 256).reshape(1, -1)
    first = own_part(own_start, hidden, gain, rstd, cot, codes, scales, rstd)
    slots = ring(piece, n)
    cots = [cot] + [slots[s] for s in range(1, n)]

    def rows_to_owners(k, after):
        (rows,) = gate([sends[k]], after)
        return lax.all_to_all(rows, "node", split_axis=0, concat_axis=0, tiled=True)

    got = [rows_to_owners(0, [slots[1], slots[n - 1], first[2]])]

    mine = jnp.concatenate([slots[s][tokens:] for s in range(1, n)], axis=0)
    weights, bits, bit = [mine], [(0, 0)], 2
    if pieces >= 8:
        one, two = flip(mine, (2, 4)), flip(mine, (4, 2))
        weights += [one, two, flip(one, (4, 2))]
        bits += [(2, 4), (4, 2), (6, 6)]
        bit = 8
    while bit < pieces:
        weights += [flip(w, (bit, bit)) for w in weights]
        bits += [(e ^ bit, o ^ bit) for e, o in bits]
        bit *= 2
    if pieces > 1:
        weights = [x for w in weights for x in (w, flip(w, (1, 1)))]
        bits = [x for e, o in bits for x in ((e, o), (o ^ 1, e ^ 1))]
    at = [lax.bitwise_xor(here, jnp.where(core == 0, even, odd)) * size for even, odd in bits]
    slot_at = jnp.stack([lax.rem(z + n - s, n) * (d // n) for s in range(1, n)])
    starts = jnp.stack(at).astype(jnp.int32)[:, None] + slot_at.astype(jnp.int32)[None, :]

    got.append(rows_to_owners(1, [got[0], mine]))
    split = max(1, len(weights) - 2)
    more_start, last_start = starts[:split], starts[split:]
    chunks = cuts(own)
    theirs, ours, parts = [], [], []

    def node_sums(k, cores, after):
        return node_sum(z, chip, cores, got[k], cots, m, after)

    def to_owners(k):
        size = chunks[k][1]
        both = [
            ours[k][p * size : (p + 1) * size].astype(F32) + theirs[k][p * size : (p + 1) * size].astype(F32)
            for p in range(m // 2)
        ]
        return [both[0]] + [flip(both[p].astype(BF16), (2 * p, 2 * p)) for p in range(1, m // 2)]

    dp_steps = m.bit_length() - 1
    node_steps = n.bit_length() - 1
    after = [got[0]]
    for k in range(len(chunks)):
        if k < len(chunks) - 1:
            away, keep = node_sums(k, [1 - core, core], after)
            away = flip(away, (1, 1))
        else:
            (away,) = node_sums(k, [1 - core], after)
            away = flip(away, (1, 1))
            (keep,) = node_sums(k, [core], after)
        theirs.append(away)
        ours.append(keep)
        after = [keep]
        if k == 0:
            got.append(rows_to_owners(2, [got[1], keep]))
            weights[split - 1 : split] = gate(weights[split - 1 : split], [keep])
            more = more_part(more_start, hidden, gain, rstd, cot, first[:3], weights[:split], size)
            after = [more[2], away]
        if k == 1:
            got.append(rows_to_owners(3, [got[2], keep]))
            weights[split : split + 1] = gate(weights[split : split + 1], [keep, *parts[0][1:]])
            values, gains, input_gradient = last_part(
                last_start,
                [own_start, more_start],
                hidden,
                gain,
                rstd,
                cot,
                more[:3],
                [first[3], more[3]],
                weights[split:],
                size,
            )
            after = [gains, away]
        if k == 2:
            gains = exchange_sum(gains, "node", n, 0, node_steps)
            gains = exchange_sum(gains, "dp", m, 0, dp_steps)
            after += [*parts[1][1:]]
        parts.append(to_owners(k))
    scale = 1.0 / (m * n)
    gain_gradient_mean = gains.reshape(d) * scale
    done = [pair_sum([x.astype(F32) for x in part]) * scale for part in parts]
    weight_grad = jnp.concatenate(done, axis=0)
    return (values, input_gradient, weight_grad, gain_gradient_mean)


def solution(mesh):
    rows = P(("dp", "node"), None)
    return jax.shard_map(
        local,
        mesh=mesh,
        in_specs=(rows, P(), P("node", None), P("node", None), rows),
        out_specs=(rows, rows, rows, P()),
        check_vma=False,
    )
```

```python
import functools

import jax
import jax.numpy as jnp
from jax import lax
from jax.experimental import pallas as pl
from jax.experimental.pallas import tpu as pltpu
from jax.sharding import PartitionSpec as P

BLOCK = 256
F32 = jnp.float32
BF16 = jnp.bfloat16
VMEM = pl.BlockSpec(memory_space=pltpu.VMEM)
SMEM = pl.BlockSpec(memory_space=pltpu.SMEM)
CHEAP = pl.CostEstimate(flops=1000, bytes_accessed=1000, transcendentals=0)
PARAMS = pltpu.CompilerParams(vmem_limit_bytes=56 * 1024 * 1024)


def cuts(own):
    units = own // 16
    last = max(1, units // 8)
    sizes = [16 * (units // 2), 16 * (units - units // 2 - last), 16 * last]
    return [(sum(sizes[:k]), size) for k, size in enumerate(sizes)]


def scaled(codes, scales):
    parts = [
        (codes[:, j * BLOCK : (j + 1) * BLOCK].astype(F32) * scales[:, j : j + 1]).astype(BF16)
        for j in range(codes.shape[1] // BLOCK)
    ]
    return jnp.concatenate(parts, axis=1)


def clipped(block):
    mean = jnp.sum(block * block, axis=-1, keepdims=True) * (1.0 / BLOCK) + 1e-06
    limit = 7.0 * (mean * lax.rsqrt(mean) * (1.0 / 3.5)).astype(BF16).astype(F32)
    return jnp.clip(block, -limit, limit)


def piece_kernel(which, codes, scales, cot, out, copy):
    out[...] = scaled(codes[...], scales[...].T)
    copy[...] = cot[...]


def weight_piece(which, codes, scales, cot, rows):
    tokens, kv = cot.shape
    return pl.pallas_call(
        piece_kernel,
        grid_spec=pltpu.PrefetchScalarGridSpec(
            num_scalar_prefetch=1,
            grid=(1,),
            in_specs=[
                pl.BlockSpec((rows, kv), lambda i, w: (w[0], 0)),
                pl.BlockSpec((scales.shape[0], rows), lambda i, w: (0, w[0])),
                pl.BlockSpec((tokens, kv), lambda i, w: (0, 0)),
            ],
            out_specs=[
                pl.BlockSpec((rows, kv), lambda i, w: (0, 0)),
                pl.BlockSpec((tokens, kv), lambda i, w: (0, 0)),
            ],
        ),
        out_shape=[jax.ShapeDtypeStruct((rows, kv), BF16), jax.ShapeDtypeStruct((tokens, kv), BF16)],
        compiler_params=PARAMS,
        cost_estimate=CHEAP,
        name="weight_piece",
    )(which, codes, scales, cot)


def norm_kernel(n, m, hidden, gain, after, *rest):
    outs, rstd, turned = rest[:-2], rest[-2], rest[-1]
    tokens, d = hidden.shape
    own = d // (n * m)
    wide = 512

    def square(i, total):
        h = hidden[:, pl.ds(pl.multiple_of(i * wide, wide), wide)].astype(F32)
        return total + jnp.sum(h * h, axis=-1, keepdims=True)

    total = lax.fori_loop(0, d // wide, square, jnp.zeros((tokens, 1), F32))
    inverse = lax.rsqrt(total * (1.0 / d) + 1e-05)
    rstd[...] = jnp.broadcast_to(inverse, rstd.shape)

    def turn(i, carry):
        at = pl.ds(pl.multiple_of(i * 256, 256), 256)
        x = hidden[:, at].astype(F32) * inverse * gain[:, at]
        turned[at, :] = x.astype(BF16).T
        return carry

    lax.fori_loop(0, d // 256, turn, 0)
    for k, (first, part) in enumerate(cuts(own)):
        for z in range(n):
            for a in range(m):
                start = (a * n + z) * own + first
                outs[k][z, a * part : (a + 1) * part, :] = turned[start : start + part, :]


def norm_rows(hidden, gain, after, n, m):
    tokens, d = hidden.shape
    parts = [jax.ShapeDtypeStruct((n, m * part, tokens), BF16) for _, part in cuts(d // (n * m))]
    got = pl.pallas_call(
        functools.partial(norm_kernel, n, m),
        in_specs=[VMEM, VMEM, pl.BlockSpec(memory_space=pl.ANY)],
        out_specs=[VMEM] * (len(parts) + 1),
        out_shape=parts + [jax.ShapeDtypeStruct((tokens, 128), F32)],
        scratch_shapes=[pltpu.VMEM((d, tokens), BF16)],
        compiler_params=PARAMS,
        cost_estimate=CHEAP,
        name="norm_rows",
    )(hidden, gain, after)
    return list(got[:-1]), got[-1]


def grad_kernel(n, m, count, me, rows, *refs):
    cots, outs = refs[:n], refs[n + count :]
    part = rows.shape[1] // m
    for which, out in enumerate(outs):
        owners = [lax.bitwise_xor(me[1], p) * 2 + me[2 + which] for p in range(m // 2)]
        lhs = []
        for s in range(n):
            source = lax.rem(me[0] + n - s, n)
            lhs.append(
                jnp.concatenate(
                    [rows[source, pl.ds(pl.multiple_of(o * part, part), part), :] for o in owners], axis=0
                )
            )
        for j in range(out.shape[1] // BLOCK):
            at = slice(j * BLOCK, (j + 1) * BLOCK)
            total = None
            for s in range(n):
                term = clipped(jnp.dot(lhs[s], cots[s][:, at], preferred_element_type=F32))
                total = term if total is None else total + term
            out[:, at] = clipped(total).astype(BF16)


def node_sum(z, chip, cores, rows, cots, m, after):
    n, count, tokens = rows.shape
    kv = cots[0].shape[1]
    return pl.pallas_call(
        functools.partial(grad_kernel, n, m, len(after)),
        in_specs=[SMEM, VMEM]
        + [VMEM] * n
        + [pl.BlockSpec(memory_space=pl.ANY)] * len(after),
        out_specs=[VMEM] * len(cores),
        out_shape=[jax.ShapeDtypeStruct((count // 2, kv), BF16)] * len(cores),
        compiler_params=PARAMS,
        cost_estimate=CHEAP,
        name="node_sum",
    )(jnp.stack([z, chip, *cores]).astype(jnp.int32), rows, *cots, *after)


def project(starts, hidden, gain, rstd, cot, weights, values, gains, mean, keep):
    for which, (tile, count, load) in enumerate(weights):
        for j in range(count):
            w = load(j * tile, tile)
            at = pl.ds(pl.multiple_of(starts[which, j], 128), tile)
            g = gain[:, at]
            xhat = hidden[:, at].astype(F32) * rstd
            normed = (xhat * g).astype(BF16)
            values[...] += jnp.dot(normed, w, preferred_element_type=F32)
            grad = lax.dot_general(
                cot[...], w, (((1,), (1,)), ((), ())), preferred_element_type=F32
            ).astype(BF16)
            keep(which, j, tile, grad)
            product = grad.astype(F32) * xhat
            gains[:, at] = jnp.sum(product, axis=0, keepdims=True)
            mean[...] += jnp.sum(product * g, axis=-1, keepdims=True)


def own_kernel(starts, hidden, gain, rstd, cot, codes, scales, after, values, gains, mean, grads):
    values[...] = jnp.zeros_like(values)
    mean[...] = jnp.zeros_like(mean)
    gains[...] = jnp.zeros_like(gains)
    tile = 256
    count = codes.shape[0] // tile

    def load(first, size):
        return scaled(codes[first : first + size, :], scales[:, first : first + size].T)

    def keep(which, j, size, grad):
        grads[:, j * size : (j + 1) * size] = grad

    project(starts, hidden, gain, rstd[:, :1], cot, [(tile, count, load)], values, gains, mean, keep)


def part_shapes(tokens, kv, d, width):
    return [
        jax.ShapeDtypeStruct((tokens, kv), F32),
        jax.ShapeDtypeStruct((1, d), F32),
        jax.ShapeDtypeStruct((tokens, 128), F32),
        jax.ShapeDtypeStruct((tokens, width), BF16),
    ]


def own_part(starts, hidden, gain, rstd, cot, codes, scales, after):
    tokens, d = hidden.shape
    return pl.pallas_call(
        own_kernel,
        in_specs=[SMEM] + [VMEM] * 6 + [pl.BlockSpec(memory_space=pl.ANY)],
        out_specs=[VMEM] * 4,
        out_shape=part_shapes(tokens, cot.shape[1], d, codes.shape[0]),
        compiler_params=PARAMS,
        cost_estimate=CHEAP,
        name="own_part",
    )(starts, hidden, gain, rstd, cot, codes, scales, after)


def listed(weights, slot):
    return [
        (slot, w.shape[0] // slot, functools.partial(lambda w, first, size: w[first : first + size, :], w))
        for w in weights
    ]


def more_kernel(count, slot, starts, hidden, gain, rstd, cot, values_in, gains_in, mean_in, *refs):
    weights, (values, gains, mean, grads) = refs[:count], refs[count:]
    values[...] = values_in[...]
    gains[...] = gains_in[...]
    mean[...] = mean_in[...]
    width = weights[0].shape[0]

    def keep(which, j, size, grad):
        grads[:, which * width + j * size : which * width + (j + 1) * size] = grad

    project(starts, hidden, gain, rstd[:, :1], cot, listed(weights, slot), values, gains, mean, keep)


def more_part(starts, hidden, gain, rstd, cot, sums, weights, slot):
    tokens, d = hidden.shape
    count = len(weights)
    return pl.pallas_call(
        functools.partial(more_kernel, count, slot),
        in_specs=[SMEM] + [VMEM] * (7 + count),
        out_specs=[VMEM] * 4,
        out_shape=part_shapes(tokens, cot.shape[1], d, count * weights[0].shape[0]),
        compiler_params=PARAMS,
        cost_estimate=CHEAP,
        name="more_part",
    )(starts, hidden, gain, rstd, cot, *sums, *weights)


def last_kernel(count, kept, slot, *refs):
    starts, others, refs = refs[0], refs[1 : 1 + kept], refs[1 + kept :]
    hidden, gain, rstd, cot, values_in, gains_in, mean_in = refs[:7]
    olds, weights = refs[7 : 7 + kept], refs[7 + kept : 7 + kept + count]
    values, gains, result, total, mean, grads = refs[7 + kept + count :]
    total[...] = values_in[...]
    gains[...] = gains_in[...]
    mean[...] = mean_in[...]
    inverse = rstd[:, :1]
    width = weights[0].shape[0]

    def keep(which, j, size, grad):
        grads[:, which * width + j * size : which * width + (j + 1) * size] = grad

    project(starts, hidden, gain, inverse, cot, listed(weights, slot), total, gains, mean, keep)
    values[...] = total[...].astype(BF16)
    center = mean[:, :1] * (1.0 / hidden.shape[1])

    def finish(start, grad):
        at = pl.ds(pl.multiple_of(start, 128), grad.shape[1])
        xhat = hidden[:, at].astype(F32) * inverse
        t = gain[:, at] * grad.astype(F32)
        result[:, at] = (inverse * (t - xhat * center)).astype(BF16)

    for at, old in list(zip(others, olds)) + [(starts, grads)]:
        size = old.shape[1] // (at.shape[0] * at.shape[1])
        for i in range(at.shape[0]):
            for j in range(at.shape[1]):
                first = (i * at.shape[1] + j) * size
                finish(at[i, j], old[:, first : first + size])


def last_part(starts, others, hidden, gain, rstd, cot, sums, olds, weights, slot):
    tokens, d = hidden.shape
    kv = cot.shape[1]
    count, kept = len(weights), len(olds)
    return pl.pallas_call(
        functools.partial(last_kernel, count, kept, slot),
        in_specs=[SMEM] * (1 + kept) + [VMEM] * (7 + kept + count),
        out_specs=[VMEM] * 3,
        out_shape=[
            jax.ShapeDtypeStruct((tokens, kv), BF16),
            jax.ShapeDtypeStruct((1, d), F32),
            jax.ShapeDtypeStruct((tokens, d), BF16),
        ],
        scratch_shapes=[
            pltpu.VMEM((tokens, kv), F32),
            pltpu.VMEM((tokens, 128), F32),
            pltpu.VMEM((tokens, count * weights[0].shape[0]), BF16),
        ],
        compiler_params=PARAMS,
        cost_estimate=CHEAP,
        name="last_part",
    )(starts, *others, hidden, gain, rstd, cot, *sums, *olds, *weights)


def gate(arrays, after):
    count = len(arrays)
    anywhere = pl.BlockSpec(memory_space=pl.ANY)
    return pl.pallas_call(
        lambda *refs: None,
        in_specs=[anywhere] * (count + len(after)),
        out_specs=[anywhere] * count,
        out_shape=[jax.ShapeDtypeStruct(x.shape, x.dtype) for x in arrays],
        input_output_aliases={i: i for i in range(count)},
        name="gate",
    )(*arrays, *after)


def pair_sum(parts):
    while len(parts) > 1:
        parts = [parts[i] + parts[i + 1] for i in range(0, len(parts), 2)]
    return parts[0]


def exchange_sum(value, axis, size, first, last):
    for step in range(first, last):
        value = value + lax.ppermute(value, axis, [(i, i ^ (1 << step)) for i in range(size)])
    return value


def ring(value, n, after):
    def shift(x, by):
        return lax.ppermute(x, "node", [(i, (i + by) % n) for i in range(n)])

    slots, up, down = {}, value, value
    for s in range(1, n // 2 + 1):
        up = shift(up, 1)
        if s == 1 and after:
            (up,) = gate([up], after)
        slots[s] = up
        if n - s > s:
            down = slots[n - s] = shift(down, -1)
    return slots


def local(hidden, gain, codes, scales, cot):
    m, n = lax.axis_size("dp"), lax.axis_size("node")
    a, z = lax.axis_index("dp"), lax.axis_index("node")
    tokens, d = hidden.shape
    kv = cot.shape[1]
    own = d // (m * n)
    pieces = min(m, d // n // 128)
    size = d // n // pieces
    gain = gain.astype(F32).reshape(1, d)
    scales = scales.T
    here = lax.rem(a, pieces)
    chip, core = lax.div(a, 2), lax.rem(a, 2)

    def flip(value, bits):
        return lax.ppermute(value, "dp", [(i, i ^ bits[i % 2]) for i in range(m)])

    piece, cot_copy = weight_piece(here.reshape(1), codes, scales, cot, size)
    sends, rstd = norm_rows(hidden, gain, piece, n, m)
    own_start = (z * (d // n) + jnp.arange(d // n // 256, dtype=jnp.int32) * 256).reshape(1, -1)
    first = own_part(own_start, hidden, gain, rstd, cot, codes, scales, rstd)
    slots = ring(piece, n, [rstd])
    (cot_copy,) = gate([cot_copy], [slots[1], slots[n - 1], first[2]])
    cot_slots = ring(cot_copy, n, [])
    cots = [cot] + [cot_slots[s] for s in range(1, n)]

    def rows_to_owners(k, after):
        (rows,) = gate([sends[k]], after)
        return lax.all_to_all(rows, "node", split_axis=0, concat_axis=0, tiled=True)

    (near,) = gate([slots[1]], [first[2]])
    mine = jnp.concatenate([near] + [slots[s] for s in range(2, n)], axis=0)
    got = [rows_to_owners(0, [mine, *cots])]
    weights, bits, bit = [mine], [(0, 0)], 2
    if pieces >= 8:
        one, two = flip(mine, (2, 4)), flip(mine, (4, 2))
        weights += [one, two, flip(one, (4, 2))]
        bits += [(2, 4), (4, 2), (6, 6)]
        bit = 8
    while bit < pieces:
        weights += [flip(w, (bit, bit)) for w in weights]
        bits += [(e ^ bit, o ^ bit) for e, o in bits]
        bit *= 2
    if pieces > 1:
        weights = [x for w in weights for x in (w, flip(w, (1, 1)))]
        bits = [x for e, o in bits for x in ((e, o), (o ^ 1, e ^ 1))]
    at = [lax.bitwise_xor(here, jnp.where(core == 0, even, odd)) * size for even, odd in bits]
    slot_at = jnp.stack([lax.rem(z + n - s, n) * (d // n) for s in range(1, n)])
    starts = jnp.stack(at).astype(jnp.int32)[:, None] + slot_at.astype(jnp.int32)[None, :]

    split = max(1, len(weights) - 2)
    more_start, last_start = starts[:split], starts[split:]
    chunks = cuts(own)
    theirs, ours, parts = [], [], []

    def node_sums(k, cores, after):
        return node_sum(z, chip, cores, got[k], cots, m, after)

    def to_owners(k):
        size = chunks[k][1]
        both = [
            ours[k][p * size : (p + 1) * size].astype(F32) + theirs[k][p * size : (p + 1) * size].astype(F32)
            for p in range(m // 2)
        ]
        return [both[0]] + [flip(both[p].astype(BF16), (2 * p, 2 * p)) for p in range(1, m // 2)]

    dp_steps = m.bit_length() - 1
    node_steps = n.bit_length() - 1
    more = more_part(more_start, hidden, gain, rstd, cot, first[:3], weights[:split], size)
    weights[split : split + 1] = gate(weights[split : split + 1], [more[2]])
    values, gains, input_gradient = last_part(
        last_start,
        [own_start, more_start],
        hidden,
        gain,
        rstd,
        cot,
        more[:3],
        [first[3], more[3]],
        weights[split:],
        size,
    )
    got.append(rows_to_owners(1, [got[0], gains]))
    away, keep = node_sums(0, [1 - core, core], [gains])
    theirs.append(flip(away, (1, 1)))
    ours.append(keep)
    parts.append(to_owners(0))
    gains = exchange_sum(gains, "dp", m, 0, dp_steps)
    got.append(rows_to_owners(2, [got[1], keep, gains, *parts[0][1:]]))
    away, keep = node_sums(1, [1 - core, core], [keep])
    (gains,) = gate([gains], [got[2]])
    gains = exchange_sum(gains, "node", n, 0, node_steps)
    theirs.append(flip(away, (1, 1)))
    ours.append(keep)
    parts.append(to_owners(1))
    (away,) = node_sums(2, [1 - core], [keep])
    theirs.append(flip(away, (1, 1)))
    (keep,) = node_sums(2, [core], [away])
    ours.append(keep)
    parts.append(to_owners(2))
    scale = 1.0 / (m * n)
    gain_gradient_mean = gains.reshape(d) * scale
    done = [pair_sum([x.astype(F32) for x in part]) * scale for part in parts]
    weight_grad = jnp.concatenate(done, axis=0)
    return (values, input_gradient, weight_grad, gain_gradient_mean)


def solution(mesh):
    rows = P(("dp", "node"), None)
    return jax.shard_map(
        local,
        mesh=mesh,
        in_specs=(rows, P(), P("node", None), P("node", None), rows),
        out_specs=(rows, rows, rows, P()),
        check_vma=False,
    )
```

```python
import functools

import jax
import jax.numpy as jnp
from jax import lax
from jax.experimental import pallas as pl
from jax.experimental.pallas import tpu as pltpu
from jax.sharding import PartitionSpec as P

BLOCK = 256
F32 = jnp.float32
BF16 = jnp.bfloat16
VMEM = pl.BlockSpec(memory_space=pltpu.VMEM)
SMEM = pl.BlockSpec(memory_space=pltpu.SMEM)
CHEAP = pl.CostEstimate(flops=1000, bytes_accessed=1000, transcendentals=0)
PARAMS = pltpu.CompilerParams(vmem_limit_bytes=56 * 1024 * 1024)


def cuts(own):
    units = own // 16
    last = max(1, units // 8)
    sizes = [16 * (units // 2), 16 * (units - units // 2 - last), 16 * last]
    return [(sum(sizes[:k]), size) for k, size in enumerate(sizes)]


def scaled(codes, scales):
    parts = [
        (codes[:, j * BLOCK : (j + 1) * BLOCK].astype(F32) * scales[:, j : j + 1]).astype(BF16)
        for j in range(codes.shape[1] // BLOCK)
    ]
    return jnp.concatenate(parts, axis=1)


def clipped(block):
    mean = jnp.sum(block * block, axis=-1, keepdims=True) * (1.0 / BLOCK) + 1e-06
    limit = 7.0 * (mean * lax.rsqrt(mean) * (1.0 / 3.5)).astype(BF16).astype(F32)
    return jnp.clip(block, -limit, limit)


def piece_kernel(which, codes, scales, out):
    out[...] = scaled(codes[...], scales[...].T)


def weight_piece(which, codes, scales, rows):
    kv = codes.shape[1]
    return pl.pallas_call(
        piece_kernel,
        grid_spec=pltpu.PrefetchScalarGridSpec(
            num_scalar_prefetch=1,
            grid=(1,),
            in_specs=[
                pl.BlockSpec((rows, kv), lambda i, w: (w[0], 0)),
                pl.BlockSpec((scales.shape[0], rows), lambda i, w: (0, w[0])),
            ],
            out_specs=pl.BlockSpec((rows, kv), lambda i, w: (0, 0)),
        ),
        out_shape=jax.ShapeDtypeStruct((rows, kv), BF16),
        compiler_params=PARAMS,
        cost_estimate=CHEAP,
        name="weight_piece",
    )(which, codes, scales)


def norm_kernel(n, m, hidden, gain, cot, after, *rest):
    outs, rstd, copy, turned = rest[:-3], rest[-3], rest[-2], rest[-1]
    copy[...] = cot[...]
    tokens, d = hidden.shape
    own = d // (n * m)
    wide = 512

    def square(i, total):
        h = hidden[:, pl.ds(pl.multiple_of(i * wide, wide), wide)].astype(F32)
        return total + jnp.sum(h * h, axis=-1, keepdims=True)

    total = lax.fori_loop(0, d // wide, square, jnp.zeros((tokens, 1), F32))
    inverse = lax.rsqrt(total * (1.0 / d) + 1e-05)
    rstd[...] = jnp.broadcast_to(inverse, rstd.shape)

    def turn(i, carry):
        at = pl.ds(pl.multiple_of(i * 256, 256), 256)
        x = hidden[:, at].astype(F32) * inverse * gain[:, at]
        turned[at, :] = x.astype(BF16).T
        return carry

    lax.fori_loop(0, d // 256, turn, 0)
    for k, (first, part) in enumerate(cuts(own)):
        for z in range(n):
            for a in range(m):
                start = (a * n + z) * own + first
                outs[k][z, a * part : (a + 1) * part, :] = turned[start : start + part, :]


def norm_rows(hidden, gain, cot, after, n, m):
    tokens, d = hidden.shape
    parts = [jax.ShapeDtypeStruct((n, m * part, tokens), BF16) for _, part in cuts(d // (n * m))]
    got = pl.pallas_call(
        functools.partial(norm_kernel, n, m),
        in_specs=[VMEM, VMEM, VMEM, pl.BlockSpec(memory_space=pl.ANY)],
        out_specs=[VMEM] * (len(parts) + 2),
        out_shape=parts + [jax.ShapeDtypeStruct((tokens, 128), F32), jax.ShapeDtypeStruct(cot.shape, BF16)],
        scratch_shapes=[pltpu.VMEM((d, tokens), BF16)],
        compiler_params=PARAMS,
        cost_estimate=CHEAP,
        name="norm_rows",
    )(hidden, gain, cot, after)
    return list(got[:-2]), got[-2], got[-1]


def grad_kernel(n, m, count, me, rows, *refs):
    cots, outs = refs[:n], refs[n + count :]
    part = rows.shape[1] // m
    for which, out in enumerate(outs):
        owners = [lax.bitwise_xor(me[1], p) * 2 + me[2 + which] for p in range(m // 2)]
        lhs = []
        for s in range(n):
            source = lax.rem(me[0] + n - s, n)
            lhs.append(
                jnp.concatenate(
                    [rows[source, pl.ds(pl.multiple_of(o * part, part), part), :] for o in owners], axis=0
                )
            )
        for j in range(out.shape[1] // BLOCK):
            at = slice(j * BLOCK, (j + 1) * BLOCK)
            total = None
            for s in range(n):
                term = clipped(jnp.dot(lhs[s], cots[s][:, at], preferred_element_type=F32))
                total = term if total is None else total + term
            out[:, at] = clipped(total).astype(BF16)


def node_sum(z, chip, cores, rows, cots, m, after):
    n, count, tokens = rows.shape
    kv = cots[0].shape[1]
    return pl.pallas_call(
        functools.partial(grad_kernel, n, m, len(after)),
        in_specs=[SMEM, VMEM]
        + [VMEM] * n
        + [pl.BlockSpec(memory_space=pl.ANY)] * len(after),
        out_specs=[VMEM] * len(cores),
        out_shape=[jax.ShapeDtypeStruct((count // 2, kv), BF16)] * len(cores),
        compiler_params=PARAMS,
        cost_estimate=CHEAP,
        name="node_sum",
    )(jnp.stack([z, chip, *cores]).astype(jnp.int32), rows, *cots, *after)


def project(starts, hidden, gain, rstd, cot, weights, values, gains, mean, keep):
    for which, (tile, count, load) in enumerate(weights):
        for j in range(count):
            w = load(j * tile, tile)
            at = pl.ds(pl.multiple_of(starts[which, j], 128), tile)
            g = gain[:, at]
            xhat = hidden[:, at].astype(F32) * rstd
            normed = (xhat * g).astype(BF16)
            values[...] += jnp.dot(normed, w, preferred_element_type=F32)
            grad = lax.dot_general(
                cot[...], w, (((1,), (1,)), ((), ())), preferred_element_type=F32
            ).astype(BF16)
            keep(which, j, tile, grad)
            product = grad.astype(F32) * xhat
            gains[:, at] = jnp.sum(product, axis=0, keepdims=True)
            mean[...] += jnp.sum(product * g, axis=-1, keepdims=True)


def own_kernel(starts, hidden, gain, rstd, cot, codes, scales, after, values, gains, mean, grads):
    values[...] = jnp.zeros_like(values)
    mean[...] = jnp.zeros_like(mean)
    gains[...] = jnp.zeros_like(gains)
    tile = 256
    count = codes.shape[0] // tile

    def load(first, size):
        return scaled(codes[first : first + size, :], scales[:, first : first + size].T)

    def keep(which, j, size, grad):
        grads[:, j * size : (j + 1) * size] = grad

    project(starts, hidden, gain, rstd[:, :1], cot, [(tile, count, load)], values, gains, mean, keep)


def part_shapes(tokens, kv, d, width):
    return [
        jax.ShapeDtypeStruct((tokens, kv), F32),
        jax.ShapeDtypeStruct((1, d), F32),
        jax.ShapeDtypeStruct((tokens, 128), F32),
        jax.ShapeDtypeStruct((tokens, width), BF16),
    ]


def own_part(starts, hidden, gain, rstd, cot, codes, scales, after):
    tokens, d = hidden.shape
    return pl.pallas_call(
        own_kernel,
        in_specs=[SMEM] + [VMEM] * 6 + [pl.BlockSpec(memory_space=pl.ANY)],
        out_specs=[VMEM] * 4,
        out_shape=part_shapes(tokens, cot.shape[1], d, codes.shape[0]),
        compiler_params=PARAMS,
        cost_estimate=CHEAP,
        name="own_part",
    )(starts, hidden, gain, rstd, cot, codes, scales, after)


def listed(weights, slot):
    return [
        (slot, w.shape[0] // slot, functools.partial(lambda w, first, size: w[first : first + size, :], w))
        for w in weights
    ]


def more_kernel(count, slot, starts, hidden, gain, rstd, cot, values_in, gains_in, mean_in, *refs):
    weights, (values, gains, mean, grads) = refs[:count], refs[count:]
    values[...] = values_in[...]
    gains[...] = gains_in[...]
    mean[...] = mean_in[...]
    width = weights[0].shape[0]

    def keep(which, j, size, grad):
        grads[:, which * width + j * size : which * width + (j + 1) * size] = grad

    project(starts, hidden, gain, rstd[:, :1], cot, listed(weights, slot), values, gains, mean, keep)


def more_part(starts, hidden, gain, rstd, cot, sums, weights, slot):
    tokens, d = hidden.shape
    count = len(weights)
    return pl.pallas_call(
        functools.partial(more_kernel, count, slot),
        in_specs=[SMEM] + [VMEM] * (7 + count),
        out_specs=[VMEM] * 4,
        out_shape=part_shapes(tokens, cot.shape[1], d, count * weights[0].shape[0]),
        compiler_params=PARAMS,
        cost_estimate=CHEAP,
        name="more_part",
    )(starts, hidden, gain, rstd, cot, *sums, *weights)


def last_kernel(count, kept, slot, *refs):
    starts, others, refs = refs[0], refs[1 : 1 + kept], refs[1 + kept :]
    hidden, gain, rstd, cot, values_in, gains_in, mean_in = refs[:7]
    olds, weights = refs[7 : 7 + kept], refs[7 + kept : 7 + kept + count]
    values, gains, result, total, mean, grads = refs[7 + kept + count :]
    total[...] = values_in[...]
    gains[...] = gains_in[...]
    mean[...] = mean_in[...]
    inverse = rstd[:, :1]
    width = weights[0].shape[0]

    def keep(which, j, size, grad):
        grads[:, which * width + j * size : which * width + (j + 1) * size] = grad

    project(starts, hidden, gain, inverse, cot, listed(weights, slot), total, gains, mean, keep)
    values[...] = total[...].astype(BF16)
    center = mean[:, :1] * (1.0 / hidden.shape[1])

    def finish(start, grad):
        at = pl.ds(pl.multiple_of(start, 128), grad.shape[1])
        xhat = hidden[:, at].astype(F32) * inverse
        t = gain[:, at] * grad.astype(F32)
        result[:, at] = (inverse * (t - xhat * center)).astype(BF16)

    for at, old in list(zip(others, olds)) + [(starts, grads)]:
        size = old.shape[1] // (at.shape[0] * at.shape[1])
        for i in range(at.shape[0]):
            for j in range(at.shape[1]):
                first = (i * at.shape[1] + j) * size
                finish(at[i, j], old[:, first : first + size])


def last_part(starts, others, hidden, gain, rstd, cot, sums, olds, weights, slot):
    tokens, d = hidden.shape
    kv = cot.shape[1]
    count, kept = len(weights), len(olds)
    return pl.pallas_call(
        functools.partial(last_kernel, count, kept, slot),
        in_specs=[SMEM] * (1 + kept) + [VMEM] * (7 + kept + count),
        out_specs=[VMEM] * 3,
        out_shape=[
            jax.ShapeDtypeStruct((tokens, kv), BF16),
            jax.ShapeDtypeStruct((1, d), F32),
            jax.ShapeDtypeStruct((tokens, d), BF16),
        ],
        scratch_shapes=[
            pltpu.VMEM((tokens, kv), F32),
            pltpu.VMEM((tokens, 128), F32),
            pltpu.VMEM((tokens, count * weights[0].shape[0]), BF16),
        ],
        compiler_params=PARAMS,
        cost_estimate=CHEAP,
        name="last_part",
    )(starts, *others, hidden, gain, rstd, cot, *sums, *olds, *weights)


def gate(arrays, after):
    count = len(arrays)
    anywhere = pl.BlockSpec(memory_space=pl.ANY)
    return pl.pallas_call(
        lambda *refs: None,
        in_specs=[anywhere] * (count + len(after)),
        out_specs=[anywhere] * count,
        out_shape=[jax.ShapeDtypeStruct(x.shape, x.dtype) for x in arrays],
        input_output_aliases={i: i for i in range(count)},
        name="gate",
    )(*arrays, *after)


def pair_sum(parts):
    while len(parts) > 1:
        parts = [parts[i] + parts[i + 1] for i in range(0, len(parts), 2)]
    return parts[0]


def exchange_sum(value, axis, size, first, last):
    for step in range(first, last):
        value = value + lax.ppermute(value, axis, [(i, i ^ (1 << step)) for i in range(size)])
    return value


def ring(value, n, after):
    def shift(x, by):
        return lax.ppermute(x, "node", [(i, (i + by) % n) for i in range(n)])

    slots, up, down = {}, value, value
    for s in range(1, n // 2 + 1):
        up = shift(up, 1)
        if s == 1 and after:
            (up,) = gate([up], after)
        slots[s] = up
        if n - s > s:
            down = slots[n - s] = shift(down, -1)
    return slots


def local(hidden, gain, codes, scales, cot):
    m, n = lax.axis_size("dp"), lax.axis_size("node")
    a, z = lax.axis_index("dp"), lax.axis_index("node")
    tokens, d = hidden.shape
    kv = cot.shape[1]
    own = d // (m * n)
    pieces = min(m, d // n // 128)
    size = d // n // pieces
    gain = gain.astype(F32).reshape(1, d)
    scales = scales.T
    here = lax.rem(a, pieces)
    chip, core = lax.div(a, 2), lax.rem(a, 2)

    def flip(value, bits):
        return lax.ppermute(value, "dp", [(i, i ^ bits[i % 2]) for i in range(m)])

    piece = weight_piece(here.reshape(1), codes, scales, size)
    sends, rstd, cot_copy = norm_rows(hidden, gain, cot, piece, n, m)
    own_start = (z * (d // n) + jnp.arange(d // n // 256, dtype=jnp.int32) * 256).reshape(1, -1)
    first = own_part(own_start, hidden, gain, rstd, cot, codes, scales, rstd)
    slots = ring(piece, n, [rstd])
    (cot_copy,) = gate([cot_copy], [slots[1], slots[n - 1], first[2]])
    cot_slots = ring(cot_copy, n, [])
    cots = [cot] + [cot_slots[s] for s in range(1, n)]

    def rows_to_owners(k, after):
        (rows,) = gate([sends[k]], after)
        return lax.all_to_all(rows, "node", split_axis=0, concat_axis=0, tiled=True)

    (near,) = gate([slots[1]], [first[2]])
    mine = jnp.concatenate([near] + [slots[s] for s in range(2, n)], axis=0)
    got = [rows_to_owners(0, [mine, *cots])]
    weights, bits, bit = [mine], [(0, 0)], 2
    if pieces >= 8:
        one, two = flip(mine, (2, 4)), flip(mine, (4, 2))
        weights += [one, two, flip(one, (4, 2))]
        bits += [(2, 4), (4, 2), (6, 6)]
        bit = 8
    while bit < pieces:
        weights += [flip(w, (bit, bit)) for w in weights]
        bits += [(e ^ bit, o ^ bit) for e, o in bits]
        bit *= 2
    if pieces > 1:
        weights = [x for w in weights for x in (w, flip(w, (1, 1)))]
        bits = [x for e, o in bits for x in ((e, o), (o ^ 1, e ^ 1))]
    at = [lax.bitwise_xor(here, jnp.where(core == 0, even, odd)) * size for even, odd in bits]
    slot_at = jnp.stack([lax.rem(z + n - s, n) * (d // n) for s in range(1, n)])
    starts = jnp.stack(at).astype(jnp.int32)[:, None] + slot_at.astype(jnp.int32)[None, :]

    split = max(1, len(weights) - 2)
    more_start, last_start = starts[:split], starts[split:]
    chunks = cuts(own)
    theirs, ours, parts = [], [], []

    def node_sums(k, cores, after):
        return node_sum(z, chip, cores, got[k], cots, m, after)

    def to_owners(k):
        size = chunks[k][1]
        both = [
            ours[k][p * size : (p + 1) * size].astype(F32) + theirs[k][p * size : (p + 1) * size].astype(F32)
            for p in range(m // 2)
        ]
        return [both[0]] + [flip(both[p].astype(BF16), (2 * p, 2 * p)) for p in range(1, m // 2)]

    dp_steps = m.bit_length() - 1
    node_steps = n.bit_length() - 1
    more = more_part(more_start, hidden, gain, rstd, cot, first[:3], weights[:split], size)
    weights[split : split + 1] = gate(weights[split : split + 1], [more[2]])
    values, gains, input_gradient = last_part(
        last_start,
        [own_start, more_start],
        hidden,
        gain,
        rstd,
        cot,
        more[:3],
        [first[3], more[3]],
        weights[split:],
        size,
    )
    got.append(rows_to_owners(1, [got[0], gains]))
    away, keep = node_sums(0, [1 - core, core], [gains])
    theirs.append(flip(away, (1, 1)))
    ours.append(keep)
    parts.append(to_owners(0))
    gains = exchange_sum(gains, "dp", m, 0, dp_steps)
    got.append(rows_to_owners(2, [got[1], keep, gains, *parts[0][1:]]))
    away, keep = node_sums(1, [1 - core, core], [keep])
    (gains,) = gate([gains], [got[2]])
    gains = exchange_sum(gains, "node", n, 0, node_steps)
    theirs.append(flip(away, (1, 1)))
    ours.append(keep)
    parts.append(to_owners(1))
    away, keep = node_sums(2, [1 - core, core], [keep])
    theirs.append(flip(away, (1, 1)))
    ours.append(keep)
    parts.append(to_owners(2))
    scale = 1.0 / (m * n)
    gain_gradient_mean = gains.reshape(d) * scale
    done = [pair_sum([x.astype(F32) for x in part]) * scale for part in parts]
    weight_grad = jnp.concatenate(done, axis=0)
    return (values, input_gradient, weight_grad, gain_gradient_mean)


def solution(mesh):
    rows = P(("dp", "node"), None)
    return jax.shard_map(
        local,
        mesh=mesh,
        in_specs=(rows, P(), P("node", None), P("node", None), rows),
        out_specs=(rows, rows, rows, P()),
        check_vma=False,
    )
```
